32 devices in a mesh: pipe: 4 (over y, x), seq: 8 (over z, core).
Axes of the slice: x: 2, y: 2, z: 4, core: 2. Of those that a mesh axis runs over, the one named last changes fastest.
Arguments:
- inputs: bfloat16 [4, 2, 1024, 1024], P('pipe', None, 'seq'), may hold values from -6 to 6
- incoming: bfloat16 [4, 2, 1024, 1024], P('pipe', None, 'seq'), may hold values from -6 to 6
- angles: float32 [4, 2, 1024], P('pipe'), may hold values from -3.140625 to 3.140625
- level_weights: float32 [4, 11, 1024], P('pipe'), may hold values from -1.75 to 1.75
- mix_weight: bfloat16 [4, 1024, 2048], P('pipe'), may hold values from -0.1875 to 0.1875
Outputs:
- grad_input: bfloat16 [4, 2, 1024, 1024], P('pipe', None, 'seq')
- grad_angles: float32 [4, 2, 1024], P('pipe')
- grad_levels: float32 [4, 11, 1024], P('pipe')
- grad_mix: float32 [4, 1024, 2048], P('pipe', 'seq')
The draws below stay inside these ranges and needn't reach their ends.
All inputs are finite; a program needn't handle non-finite values.
Results may differ from the reference program's by a relative error of at most 0.015.
Values may be sent and summed in bfloat16 or wider, within the bound.
A program may use at most 128 MiB of HBM per device.

```python
import jax
import jax.numpy as jnp
from jax import lax

D = 1024
BATCH = 2
SEQ = 1024
LEVELS = 10
N_PIPE = 4


def spiked(result, own_key, source, target, blocks, factor):
    def block_of(dim):
        return (jnp.arange(result.shape[dim]) // (result.shape[dim] // blocks)).reshape((-1,) + (1,) * (result.ndim - 1 - dim))

    one_side = jax.random.permutation(own_key, blocks)[block_of(target)]
    far = (block_of(target) + blocks // 2) % blocks
    return jnp.where((block_of(source) == one_side) | (block_of(source) == far), factor * result, result)


def levels(stream_key, shape, cuts, least, top_value):
    gain, own = 1.0, jax.random.fold_in(stream_key, 6)
    for axis_at, shards_of in cuts:
        heights = jnp.exp(jax.random.uniform(jax.random.fold_in(own, axis_at), (shards_of,), jnp.float32, least / len(cuts), top_value / len(cuts)))
        gain = gain * jnp.repeat(heights, shape[axis_at] // shards_of).reshape([-1 if axis == axis_at else 1 for axis in range(len(shape))])
    return gain


def bell_draw(stream_key, dims, width, reach, shards=(), held_as=jnp.bfloat16):
    result = jax.random.normal(stream_key, dims, jnp.float32) * width
    if len(shards) > 0:
        result = levels(stream_key, dims, shards, -0.22, 0.18) * result
    return jnp.clip(result, min=-reach, max=reach).astype(held_as)


def heavy_noise(key, dims, spread, most, split, heavy, dtype=jnp.bfloat16):
    entries = spread * jax.random.normal(key, dims, jnp.float32)
    if split:
        entries = entries * levels(key, dims, split, -0.22, 0.18)
    return jnp.clip(spiked(entries, jax.random.fold_in(key, 3), *heavy), -most, most).astype(dtype)


def setup_inputs(seed: int = 0) -> dict:
    key_of = jax.random.split(jax.random.key(seed), 6)
    return {
        "inputs": heavy_noise(key_of[0], (N_PIPE, BATCH, SEQ, D), 1.0, 6.0, ((0, 4), (2, 8)), (2, 3, 8, 2.0)),
        "incoming": bell_draw(key_of[1], (N_PIPE, BATCH, SEQ, D), 1.0, 6.0, ((0, 4), (2, 8))),
        "angles": jnp.clip(jax.random.uniform(key_of[2], (N_PIPE, 2, D), jnp.float32, -3.140625, 3.140625), -3.140625, 3.140625),
        "level_weights": bell_draw(key_of[3], (N_PIPE, LEVELS + 1, D), (LEVELS + 1) ** -0.5, 1.75, ((0, 4),), jnp.float32),
        "mix_weight": bell_draw(key_of[4], (N_PIPE, D, 2 * D), D ** -0.5, 0.1875, ((0, 4),)),
    }


def rounded(values):
    return lax.optimization_barrier(values.astype(jnp.bfloat16))

def behind(values, spacing):
    return jnp.pad(values, ((0, 0), (spacing, 0), (0, 0)))[:, :values.shape[1], :]

def from_later(values, spacing):
    return jnp.pad(values, ((0, 0), (0, spacing), (0, 0)))[:, spacing:, :]

def section(activations, cotangent, angle_pair, weights, w_mix):
    grad_scale = float(BATCH * SEQ) ** (-0.5)
    c_low = jnp.cos(angle_pair[0])
    s_low = jnp.sin(angle_pair[0])
    c_high = jnp.cos(angle_pair[1])
    s_high = jnp.sin(angle_pair[1])
    state_now = activations
    states = []
    mixed = jnp.zeros(activations.shape, jnp.float32)
    for level_idx in range(LEVELS):
        spacing = 2 ** level_idx
        current = state_now.astype(jnp.float32)
        previous = behind(current, spacing)
        mixed = mixed + weights[level_idx] * (c_high * current + s_high * previous)
        states.append(state_now)
        state_now = rounded(c_low * current + s_low * previous)
    top_state = state_now.astype(jnp.float32)
    mixed = mixed + weights[LEVELS] * top_state
    activated = jax.nn.gelu(mixed).astype(jnp.bfloat16).reshape(-1, D)
    projected = jnp.dot(activated, w_mix, preferred_element_type=jnp.float32)
    value_half = projected[:, :D]
    gate_value = jax.nn.sigmoid(projected[:, D:])
    upstream = cotangent.reshape(-1, D).astype(jnp.float32)
    grad_proj = jnp.concatenate([upstream * gate_value, upstream * value_half * gate_value * (1.0 - gate_value)], axis=1).astype(jnp.bfloat16)
    grad_act = jnp.dot(grad_proj, w_mix.T, preferred_element_type=jnp.float32)
    grad_weight = jnp.dot(activated.T, grad_proj, preferred_element_type=jnp.float32) * grad_scale
    _, pullback = jax.vjp(jax.nn.gelu, mixed)
    grad_conv = pullback(grad_act.reshape(mixed.shape))[0]
    adjoint = weights[LEVELS] * grad_conv
    level_grads = [None] * (LEVELS + 1)
    level_grads[LEVELS] = lax.optimization_barrier(jnp.sum(grad_conv * top_state, axis=(0, 1)))
    zero_row = jnp.zeros((D,), jnp.float32)
    tap_low_now, tap_low_back, tap_high_now, tap_high_back = (zero_row, zero_row, zero_row, zero_row)
    for level_idx in reversed(range(LEVELS)):
        spacing = 2 ** level_idx
        current = states[level_idx].astype(jnp.float32)
        previous = behind(current, spacing)
        weighted = weights[level_idx] * grad_conv
        level_grads[level_idx] = lax.optimization_barrier(jnp.sum(grad_conv * (c_high * current + s_high * previous), axis=(0, 1)))
        tap_low_now = tap_low_now + lax.optimization_barrier(jnp.sum(adjoint * current, axis=(0, 1)))
        tap_low_back = tap_low_back + lax.optimization_barrier(jnp.sum(adjoint * previous, axis=(0, 1)))
        tap_high_now = tap_high_now + lax.optimization_barrier(jnp.sum(weighted * current, axis=(0, 1)))
        tap_high_back = tap_high_back + lax.optimization_barrier(jnp.sum(weighted * previous, axis=(0, 1)))
        carried = rounded(s_low * adjoint + s_high * weighted).astype(jnp.float32)
        adjoint = c_low * adjoint + c_high * weighted + from_later(carried, spacing)
    grad_input = (cotangent.astype(jnp.float32) + adjoint).astype(jnp.bfloat16)
    grad_angle = jnp.stack([c_low * tap_low_back - s_low * tap_low_now, c_high * tap_high_back - s_high * tap_high_now]) * grad_scale
    return (grad_input, grad_angle, jnp.stack(level_grads) * grad_scale, grad_weight)

def reference(inputs, incoming, angles, level_weights, mix_weight):
    results = []
    for section_idx in range(N_PIPE):
        results.append(section(inputs[section_idx], incoming[(section_idx + 1) % N_PIPE], angles[section_idx], level_weights[section_idx], mix_weight[section_idx]))
    return (jnp.stack([item[0] for item in results]), jnp.stack([item[1] for item in results]), jnp.stack([item[2] for item in results]), jnp.stack([item[3] for item in results]))
```

```python
import functools

import jax
import jax.numpy as jnp
from jax import lax
from jax.experimental import pallas as pl
from jax.experimental.pallas import tpu as pltpu
from jax.sharding import PartitionSpec as P


def shifted_2(block, axis, distance):
    devices = range(lax.axis_size(axis))
    route = [(i - distance, i) for i in devices if i - distance in devices]
    return lax.ppermute(block, axis, route)


def shifted_3(value, axis, steps):
    count = lax.axis_size(axis)
    pairs = [(source, (source + steps) % count) for source in range(count)]
    return lax.ppermute(value, axis, pairs)


def rounded(values):
    return lax.optimization_barrier(values.astype(jnp.bfloat16))


def near_behind(state_now, spacing, positions):
    rim_rows = shifted_2(state_now[:, positions - spacing :, :], "seq", 1)
    return jnp.concatenate([rim_rows, state_now[:, : positions - spacing, :]], axis=1)


def tap_terms(totals, adjoint, weighted, current, previous):
    return (
        totals[0] + jnp.sum(adjoint * current, axis=(0, 1)),
        totals[1] + jnp.sum(adjoint * previous, axis=(0, 1)),
        totals[2] + jnp.sum(weighted * current, axis=(0, 1)),
        totals[3] + jnp.sum(weighted * previous, axis=(0, 1)),
    )


def shards_by_levels(inputs, incoming, angles, level_weights, mix_weight):
    activations = inputs[0]
    sequences, positions, channels = activations.shape
    seq_devices = lax.axis_size("seq")
    levels = level_weights.shape[1] - 1
    near_count = positions.bit_length() - 1
    grad_scale = float(sequences * positions * seq_devices) ** (-0.5)
    weights = level_weights[0]
    w_mix = mix_weight[0]
    c_low = jnp.cos(angles[0, 0])
    s_low = jnp.sin(angles[0, 0])
    c_high = jnp.cos(angles[0, 1])
    s_high = jnp.sin(angles[0, 1])
    received = shifted_3(incoming, "pipe", -1)[0]
    states = []
    shifted_states = []
    mixed = jnp.zeros(activations.shape, jnp.float32)
    state_now = activations
    for level_idx in range(near_count):
        spacing = 2**level_idx
        shifted = near_behind(state_now, spacing, positions)
        current = state_now.astype(jnp.float32)
        previous = shifted.astype(jnp.float32)
        mixed = mixed + weights[level_idx] * (c_high * current + s_high * previous)
        states.append(state_now)
        shifted_states.append(shifted)
        state_now = rounded(c_low * current + s_low * previous)
    for level_idx in range(near_count, levels):
        spacing = 2**level_idx
        shifted = shifted_2(state_now, "seq", spacing // positions)
        current = state_now.astype(jnp.float32)
        previous = shifted.astype(jnp.float32)
        mixed = mixed + weights[level_idx] * (c_high * current + s_high * previous)
        states.append(state_now)
        shifted_states.append(shifted)
        state_now = rounded(c_low * current + s_low * previous)
    top_state = state_now.astype(jnp.float32)
    mixed = mixed + weights[levels] * top_state
    activated = jax.nn.gelu(mixed).astype(jnp.bfloat16).reshape(-1, channels)
    projected = jnp.dot(activated, w_mix, preferred_element_type=jnp.float32)
    value_half = projected[:, :channels]
    gate_value = jax.nn.sigmoid(projected[:, channels:])
    upstream = received.reshape(-1, channels).astype(jnp.float32)
    grad_proj = jnp.concatenate(
        [upstream * gate_value, upstream * value_half * gate_value * (1.0 - gate_value)], axis=1
    ).astype(jnp.bfloat16)
    grad_act = jnp.einsum("rk,ck->rc", grad_proj, w_mix, preferred_element_type=jnp.float32)
    grad_weight = (
        lax.psum_scatter(
            jnp.einsum("rc,rk->ck", activated, grad_proj, preferred_element_type=jnp.float32),
            "seq",
            scatter_dimension=0,
            tiled=True,
        )
        * grad_scale
    )
    _, pullback = jax.vjp(jax.nn.gelu, mixed)
    grad_conv = pullback(grad_act.reshape(mixed.shape))[0]
    level_grads = [None] * (levels + 1)
    adjoint = weights[levels] * grad_conv
    level_grads[levels] = jnp.sum(grad_conv * top_state, axis=(0, 1))
    zero_row = jnp.zeros((channels,), jnp.float32)
    totals = (zero_row, zero_row, zero_row, zero_row)
    for level_idx in reversed(range(near_count, levels)):
        spacing = 2**level_idx
        current = states[level_idx].astype(jnp.float32)
        previous = shifted_states[level_idx].astype(jnp.float32)
        weighted = weights[level_idx] * grad_conv
        level_grads[level_idx] = jnp.sum(
            grad_conv * (c_high * current + s_high * previous), axis=(0, 1)
        )
        totals = tap_terms(totals, adjoint, weighted, current, previous)
        carried = rounded(s_low * adjoint + s_high * weighted)
        arrived = shifted_2(carried, "seq", -(spacing // positions)).astype(jnp.float32)
        adjoint = c_low * adjoint + c_high * weighted + arrived
    for level_idx in reversed(range(near_count)):
        spacing = 2**level_idx
        current = states[level_idx].astype(jnp.float32)
        previous = shifted_states[level_idx].astype(jnp.float32)
        weighted = weights[level_idx] * grad_conv
        level_grads[level_idx] = jnp.sum(
            grad_conv * (c_high * current + s_high * previous), axis=(0, 1)
        )
        totals = tap_terms(totals, adjoint, weighted, current, previous)
        carried = rounded(s_low * adjoint + s_high * weighted)
        rim_rows = shifted_2(carried[:, :spacing, :], "seq", -1)
        arrived = jnp.concatenate([carried[:, spacing:, :], rim_rows], axis=1).astype(jnp.float32)
        adjoint = c_low * adjoint + c_high * weighted + arrived
    angle_terms = jnp.stack(
        [c_low * totals[1] - s_low * totals[0], c_high * totals[3] - s_high * totals[2]]
    )
    angle_total, level_total = lax.psum((angle_terms, jnp.stack(level_grads)), "seq")
    grad_input = (received.astype(jnp.float32) + adjoint).astype(jnp.bfloat16)
    return (
        grad_input[None],
        (angle_total * grad_scale)[None],
        (level_total * grad_scale)[None],
        grad_weight[None],
    )


MESH = pl.DeviceIdType.MESH
CORES = 2
F32 = jnp.float32
BF16 = jnp.bfloat16


def whole_kernel(
    pipes, n, levels,
    x_ref, inc_ref, ang_ref, lw_ref, w_hbm,
    gin_ref, small_ref, gmix_ref,
    xin, cot, wv, actc, actf, gp, ga, gab, gac, dgelu, adjs, adjf, coef, accs, mine,
    pb, px, txr, rxr, txl, rxl, states, adjoints,
    w_sem, cot_s, cot_r, loc_sem, a_s, a_r, px_s, px_r, rs_s, rs_r,
):
    batch, rows, chans = inc_ref.shape
    seq = n * rows
    slab = chans // n
    nz = n // CORES
    me = lax.axis_index("seq")
    pipe = lax.axis_index("pipe")
    z = me // CORES
    core = me % CORES
    my_slab = pl.ds(pl.multiple_of(me * slab, slab), slab)
    my_rows = pl.ds(pl.multiple_of(me * rows, rows), rows)

    def times(d, size):
        return d * size if isinstance(d, int) else pl.multiple_of(d * size, size)

    def slab_of(d):
        return pl.ds(times(d, slab), slab)

    def rows_of(d):
        return pl.ds(times(d, rows), rows)

    w_copy = pltpu.make_async_copy(w_hbm, wv, w_sem)
    w_copy.start()

    barrier = pltpu.get_barrier_semaphore()
    for k in range(1, n):
        pl.semaphore_signal(barrier, inc=1, device_id={"seq": (me + k) % n}, device_id_type=MESH)
    for k in (1, pipes - 1):
        pl.semaphore_signal(barrier, inc=1, device_id={"pipe": (pipe + k) % pipes}, device_id_type=MESH)
    pl.semaphore_wait(barrier, n + 1)

    def to_slab(phase, src, dst, d, start):
        return pltpu.make_async_remote_copy(
            src_ref=src.at[:, :, slab_of(d)],
            dst_ref=dst.at[:, rows_of(start), :],
            send_sem=a_s.at[phase, d],
            recv_sem=a_r.at[phase, start],
            device_id={"seq": d},
            device_id_type=MESH,
        )

    def to_rows(phase, src, dst, d, start):
        return pltpu.make_async_remote_copy(
            src_ref=src.at[:, rows_of(d), :],
            dst_ref=dst.at[:, :, slab_of(start)],
            send_sem=a_s.at[phase, d],
            recv_sem=a_r.at[phase, start],
            device_id={"seq": d},
            device_id_type=MESH,
        )

    def sums_copy(d, start):
        return pltpu.make_async_remote_copy(
            src_ref=mine,
            dst_ref=small_ref.at[:, slab_of(start)],
            send_sem=a_s.at[4, d],
            recv_sem=a_r.at[4, start],
            device_id={"seq": d},
            device_id_type=MESH,
        )

    x_local = pltpu.make_async_copy(x_ref.at[:, :, my_slab], xin.at[:, my_rows, :], loc_sem.at[0])
    x_local.start()
    for k in range(1, n):
        to_slab(0, x_ref, xin, (me + k) % n, me).start()
    cot_copy = pltpu.make_async_remote_copy(
        src_ref=inc_ref, dst_ref=cot, send_sem=cot_s, recv_sem=cot_r,
        device_id={"pipe": (pipe + pipes - 1) % pipes}, device_id_type=MESH,
    )
    cot_copy.start()

    angle = ang_ref[:, my_slab]
    cosines = jnp.cos(angle)
    sines = jnp.sin(angle)
    weight = lw_ref[:, my_slab]
    c_low, c_high = cosines[0:1], cosines[1:2]
    s_low, s_high = sines[0:1], sines[1:2]
    coef[0:1, :] = c_low
    coef[1:2, :] = s_low
    for l in range(levels):
        coef[pl.ds(8 + l, 1), :] = weight[l : l + 1] * c_high
        coef[pl.ds(8 + levels + l, 1), :] = weight[l : l + 1] * s_high
    top_row = 8 + 2 * levels
    coef[pl.ds(top_row, 1), :] = weight[levels : levels + 1]
    accs[...] = jnp.zeros_like(accs)
    pads = [max(8, 2**l) for l in range(levels)]
    for l in range(levels):
        for b in range(batch):
            states[l][b, pl.ds(0, pads[l]), :] = jnp.zeros((pads[l], slab), F32)
            adjoints[l][b, pl.ds(seq, pads[l]), :] = jnp.zeros((pads[l], slab), F32)
    x_local.wait()

    root = (2.0 / 3.141592653589793) ** 0.5

    def forward(j, carry):
        @pl.when(j != me)
        def _():
            to_slab(0, x_ref, xin, me, j).wait_recv()

        base = times(j, rows)
        for b in range(batch):
            now = xin[b, pl.ds(base, rows), :].astype(F32)
            mixed = jnp.zeros((rows, slab), F32)
            for l in range(levels):
                states[l][b, pl.ds(base + pads[l], rows), :] = now
                before = states[l][b, pl.ds(base + (pads[l] - 2**l), rows), :]
                mixed = mixed + (coef[pl.ds(8 + l, 1), :] * now + coef[pl.ds(8 + levels + l, 1), :] * before)
                now = coef[0:1, :] * now + coef[1:2, :] * before
            states[levels][b, pl.ds(base, rows), :] = now
            mixed = mixed + coef[pl.ds(top_row, 1), :] * now
            square = mixed * mixed
            t = jnp.tanh(root * mixed * (1.0 + 0.044715 * square))
            half = 0.5 * (1.0 + t)
            actc[b, pl.ds(base, rows), :] = (mixed * half).astype(BF16)
            dgelu[b, pl.ds(base, rows), :] = half + (0.5 * root) * mixed * (1.0 - t * t) * (
                1.0 + (3.0 * 0.044715) * square
            )

        @pl.when(j != me)
        def _():
            to_rows(1, actc, actf, j, me).start()

        return carry

    lax.fori_loop(0, n, forward, 0)
    for b in range(batch):
        actf[b, :, my_slab] = actc[b, my_rows, :]
    w_copy.wait()
    cot_copy.wait_recv()
    for k in range(1, n):
        to_rows(1, actc, actf, me, (me + n - k) % n).wait_recv()

    tile = 256
    ga[...] = jnp.zeros_like(ga)

    def mix(i, carry):
        left = pl.ds(pl.multiple_of(i * tile, tile), tile)
        right = pl.ds(pl.multiple_of(chans + i * tile, tile), tile)
        act = actf[...].reshape(batch * rows, chans)
        w_left = wv[:, left]
        w_right = wv[:, right]
        value = jnp.dot(act, w_left, preferred_element_type=F32)
        gate = jnp.dot(act, w_right, preferred_element_type=F32)
        sig = jax.nn.sigmoid(gate)
        up = cot[:, :, left].reshape(batch * rows, tile).astype(F32) * sig
        first = up.astype(BF16)
        second = (up * value * (1.0 - sig)).astype(BF16)
        gp[:, left] = first
        gp[:, right] = second
        dims = (((1,), (1,)), ((), ()))
        ga[...] += lax.dot_general(first, w_left, dims, preferred_element_type=F32) + lax.dot_general(
            second, w_right, dims, preferred_element_type=F32
        )
        return carry

    lax.fori_loop(0, chans // tile, mix, 0)
    gab[...] = ga[...].astype(BF16).reshape(batch, rows, chans)
    for k in range(1, n):
        to_slab(2, gab, gac, (me + k) % n, me).start()
    for b in range(batch):
        gac[b, my_rows, :] = gab[b, :, my_slab]

    other = me + 1 - 2 * core
    half_rows = chans // nz // CORES
    theirs = pl.ds(pl.multiple_of((1 - core) * half_rows, half_rows), half_rows)
    ours = pl.ds(pl.multiple_of(core * half_rows, half_rows), half_rows)

    def pair_copy(q):
        return pltpu.make_async_remote_copy(
            src_ref=pb.at[q, theirs, :], dst_ref=px.at[q], send_sem=px_s.at[q], recv_sem=px_r.at[q],
            device_id={"seq": other}, device_id_type=MESH,
        )

    width = 512

    def outer_product(q, carry):
        block = pl.ds(pl.multiple_of(q * (chans // nz), chans // nz), chans // nz)

        def columns(i, carry):
            cols = pl.ds(pl.multiple_of(i * width, width), width)
            part = actf[:, :, block].reshape(batch * rows, chans // nz)
            pb[q, :, cols] = lax.dot_general(
                part, gp[:, cols], (((0,), (0,)), ((), ())), preferred_element_type=F32
            ).astype(BF16)
            return carry

        lax.fori_loop(0, 2 * chans // width, columns, 0)
        pair_copy(q).start()
        return carry

    lax.fori_loop(0, nz, outer_product, 0)

    def chain_copy(side, q):
        src, dst = ((txr, rxr), (txl, rxl))[side]
        return pltpu.make_async_remote_copy(
            src_ref=src.at[q], dst_ref=dst.at[q], send_sem=rs_s.at[side, q], recv_sem=rs_r.at[side, q],
            device_id={"seq": (me + (CORES if side == 0 else n - CORES)) % n}, device_id_type=MESH,
        )

    def summed(q, extra, into):
        def body(i, carry):
            cols = pl.ds(pl.multiple_of(i * width, width), width)
            total = pb[q, ours, cols].astype(F32) + px[q, :, cols].astype(F32)
            for e in extra:
                total = total + e[q, :, cols].astype(F32)
            into[:, cols] = total.astype(into.dtype)
            return carry

        lax.fori_loop(0, 2 * chans // width, body, 0)

    for q in range(nz):
        pair_copy(q).wait_recv()

    def send_step(step, ends):
        right_q, left_q = nz - 1 - step, step
        for side, q, goes, first in (
            (0, right_q, z < right_q, z == 0),
            (1, left_q, z > left_q, z == nz - 1),
        ):
            if ends:
                @pl.when(jnp.logical_and(goes, first))
                def _():
                    summed(q, (), (txr, txl)[side].at[q])
                    chain_copy(side, q).start()
            else:
                @pl.when(jnp.logical_and(goes, jnp.logical_not(first)))
                def _():
                    chain_copy(side, q).wait_recv()
                    summed(q, ((rxr, rxl)[side],), (txr, txl)[side].at[q])
                    chain_copy(side, q).start()

    send_step(0, True)

    def fold(values):
        return jnp.sum(values.reshape(rows // 8, 8, slab), axis=0)

    def backward(i, carry):
        j = n - 1 - i

        @pl.when(j != me)
        def _():
            to_slab(2, gab, gac, me, j).wait_recv()

        base = times(j, rows)
        for b in range(batch):
            grad = gac[b, pl.ds(base, rows), :].astype(F32) * dgelu[b, pl.ds(base, rows), :]
            accs[levels, 0] += fold(grad * states[levels][b, pl.ds(base, rows), :])
            adj = coef[pl.ds(top_row, 1), :] * grad
            for l in reversed(range(levels)):
                adjoints[l][b, pl.ds(base, rows), :] = (
                    coef[1:2, :] * adj + coef[pl.ds(8 + levels + l, 1), :] * grad
                )
                current = states[l][b, pl.ds(base + pads[l], rows), :]
                before = states[l][b, pl.ds(base + (pads[l] - 2**l), rows), :]
                accs[l, 0] += fold(grad * current)
                accs[l, 1] += fold(grad * before)
                accs[l, 2] += fold(adj * current)
                accs[l, 3] += fold(adj * before)
                carried = adjoints[l][b, pl.ds(base + 2**l, rows), :]
                adj = coef[0:1, :] * adj + coef[pl.ds(8 + l, 1), :] * grad + carried
            adjs[b, pl.ds(base, rows), :] = adj.astype(BF16)

        @pl.when(j != me)
        def _():
            to_rows(3, adjs, adjf, j, me).start()

        return carry

    for i in range(n):
        backward(i, 0)
    for b in range(batch):
        adjf[b, :, my_slab] = adjs[b, my_rows, :]

    for step in range(1, nz - 1):
        send_step(step, True)
    for step in range(nz - 1):
        send_step(step, False)

    low_now = jnp.zeros((1, slab), F32)
    low_back, high_now, high_back = low_now, low_now, low_now
    mine[...] = jnp.zeros_like(mine)

    def total(l, k):
        return jnp.sum(accs[l, k], axis=0, keepdims=True)

    for l in range(levels):
        now, back = total(l, 0), total(l, 1)
        weight_l = lw_ref[pl.ds(l, 1), my_slab]
        mine[pl.ds(l, 1), :] = c_high * now + s_high * back
        high_now = high_now + weight_l * now
        high_back = high_back + weight_l * back
        low_now = low_now + total(l, 2)
        low_back = low_back + total(l, 3)
    mine[pl.ds(levels, 1), :] = total(levels, 0)
    mine[pl.ds(levels + 1, 1), :] = c_low * low_back - s_low * low_now
    mine[pl.ds(levels + 2, 1), :] = c_high * high_back - s_high * high_now
    for k in range(1, n):
        sums_copy((me + k) % n, me).start()
    small_ref[:, my_slab] = mine[...]

    for k in range(1, n):
        to_rows(3, adjs, adjf, me, (me + n - k) % n).wait_recv()
    for b in range(batch):
        gin_ref[b] = (cot[b].astype(F32) + adjf[b].astype(F32)).astype(BF16)

    for q in range(nz):
        @pl.when(q == z)
        def _():
            if q > 0:
                chain_copy(0, q).wait_recv()
            if q < nz - 1:
                chain_copy(1, q).wait_recv()
            extra = ((rxr,) if q > 0 else ()) + ((rxl,) if q < nz - 1 else ())
            summed(q, extra, gmix_ref)

    for k in range(1, n):
        sums_copy(me, (me + n - k) % n).wait_recv()

    for k in range(1, n):
        d = (me + k) % n
        to_slab(0, x_ref, xin, d, me).wait_send()
        to_rows(1, actc, actf, d, me).wait_send()
        to_slab(2, gab, gac, d, me).wait_send()
        to_rows(3, adjs, adjf, d, me).wait_send()
        sums_copy(d, me).wait_send()
    cot_copy.wait_send()
    for q in range(nz):
        pair_copy(q).wait_send()

        @pl.when(z < q)
        def _():
            chain_copy(0, q).wait_send()

        @pl.when(z > q)
        def _():
            chain_copy(1, q).wait_send()


def shards_by_slabs(pipes, n, inputs, incoming, angles, level_weights, mix_weight):
    _, batch, rows, chans = inputs.shape
    levels = level_weights.shape[1] - 1
    seq = n * rows
    slab = chans // n
    nz = n // CORES
    grad_scale = float(batch * seq) ** (-0.5)
    small_rows = -(-(levels + 3) // 8) * 8
    pads = [max(8, 2**l) for l in range(levels)]
    vmem = pl.BlockSpec(memory_space=pltpu.VMEM)
    grid_rows = batch * rows
    block = (nz, chans // n, 2 * chans)
    grad_input, small, grad_mix = pl.pallas_call(
        functools.partial(whole_kernel, pipes, n, levels),
        out_shape=(
            jax.ShapeDtypeStruct((batch, rows, chans), BF16),
            jax.ShapeDtypeStruct((small_rows, chans), F32),
            jax.ShapeDtypeStruct((chans // n, 2 * chans), F32),
        ),
        in_specs=[vmem, vmem, vmem, vmem, pl.BlockSpec(memory_space=pl.ANY)],
        out_specs=(vmem, vmem, vmem),
        scratch_shapes=[
            pltpu.VMEM((batch, seq, slab), BF16),
            pltpu.VMEM((batch, rows, chans), BF16),
            pltpu.VMEM((chans, 2 * chans), BF16),
            pltpu.VMEM((batch, seq, slab), BF16),
            pltpu.VMEM((batch, rows, chans), BF16),
            pltpu.VMEM((grid_rows, 2 * chans), BF16),
            pltpu.VMEM((grid_rows, chans), F32),
            pltpu.VMEM((batch, rows, chans), BF16),
            pltpu.VMEM((batch, seq, slab), BF16),
            pltpu.VMEM((batch, seq, slab), F32),
            pltpu.VMEM((batch, seq, slab), BF16),
            pltpu.VMEM((batch, rows, chans), BF16),
            pltpu.VMEM((-(-(9 + 2 * levels) // 8) * 8, slab), F32),
            pltpu.VMEM((levels + 1, 4, 8, slab), F32),
            pltpu.VMEM((small_rows, slab), F32),
            pltpu.VMEM((nz, chans // nz, 2 * chans), BF16),
            pltpu.VMEM(block, BF16),
            pltpu.VMEM(block, BF16),
            pltpu.VMEM(block, BF16),
            pltpu.VMEM(block, BF16),
            pltpu.VMEM(block, BF16),
            [pltpu.VMEM((batch, pad + seq, slab), F32) for pad in pads + [0]],
            [pltpu.VMEM((batch, seq + pad, slab), F32) for pad in pads],
            pltpu.SemaphoreType.DMA,
            pltpu.SemaphoreType.DMA,
            pltpu.SemaphoreType.DMA,
            pltpu.SemaphoreType.DMA((1,)),
            pltpu.SemaphoreType.DMA((5, n)),
            pltpu.SemaphoreType.DMA((5, n)),
            pltpu.SemaphoreType.DMA((nz,)),
            pltpu.SemaphoreType.DMA((nz,)),
            pltpu.SemaphoreType.DMA((2, nz)),
            pltpu.SemaphoreType.DMA((2, nz)),
        ],
        compiler_params=pltpu.CompilerParams(
            collective_id=0, has_side_effects=True, vmem_limit_bytes=60 * 2**20
        ),
        cost_estimate=pl.CostEstimate(
            flops=12 * grid_rows * chans * chans, bytes_accessed=8 * 2**20, transcendentals=4 * grid_rows * chans
        ),
    )(inputs[0], incoming[0], angles[0], level_weights[0], mix_weight[0])
    return (
        grad_input[None],
        (small[levels + 1 : levels + 3] * grad_scale)[None],
        (small[: levels + 1] * grad_scale)[None],
        (grad_mix * grad_scale)[None],
    )


def shards_choice(pipes, n, inputs, incoming, angles, level_weights, mix_weight):
    _, _, rows, chans = inputs.shape
    levels = level_weights.shape[1] - 1
    fits = chans == 128 * n and n % CORES == 0 and pipes > 2 and rows % 16 == 0 and 2**levels <= n * rows <= 1024
    if fits:
        return shards_by_slabs(pipes, n, inputs, incoming, angles, level_weights, mix_weight)
    return shards_by_levels(inputs, incoming, angles, level_weights, mix_weight)


def solution(mesh):
    body = functools.partial(shards_choice, mesh.shape["pipe"], mesh.shape["seq"])
    placed = (
        P("pipe", None, "seq", None),
        P("pipe", None, "seq", None),
        P("pipe", None, None),
        P("pipe", None, None),
        P("pipe", None, None),
    )
    return jax.shard_map(
        body,
        mesh=mesh,
        in_specs=placed,
        out_specs=(
            P("pipe", None, "seq", None),
            P("pipe", None, None),
            P("pipe", None, None),
            P("pipe", "seq", None),
        ),
        check_vma=False,
    )
```
